256 devices in a mesh: row: 8 (over y, core), col: 32 (over x, z).
Axes of the slice: x: 4, y: 4, z: 8, core: 2. Of those that a mesh axis runs over, the one named last changes fastest.
Arguments:
- features: bfloat16 [32768, 128], P(('col', 'row')), may hold values from -6 to 6
- tile_values: bfloat16 [32768, 128, 128], P(('row', 'col')), may hold values from -0.0625 to 0.0625
- tile_rows: int32 [32768], P(('row', 'col')), may hold values from 0 to 31, as said below
- tile_cols: int32 [32768], P(('row', 'col')), may hold values from 0 to 7, as said below
- tile_count: int32 [256], P(('row', 'col')), may hold values from 16 to 128, as said below
- weight_in: bfloat16 [128, 1024], replicated, may hold values from -0.5 to 0.5
- weight_hidden: bfloat16 [1024, 1024], replicated, may hold values from -0.1875 to 0.1875
Outputs:
- hidden_out: bfloat16 [32768, 1024], P(('col', 'row'))
The draws below stay inside these ranges and needn't reach their ends.
Inputs may be any that keep to these rules, and one draw needn't show every extreme that they name: Within one device's 128 slots (live and ignored alike) the pairs (tile_rows, tile_cols) are all different; tile_rows indexes the 32 block rows of the device's row panel. tile_cols indexes the 8 block columns of the device's column panel. A device's live tiles are its first tile_count slots.
All inputs are finite; a program needn't handle non-finite values.
Results may differ from the reference program's by a relative error of at most 0.008.
Values may be sent and summed in bfloat16 or wider, within the bound.
No kernel may reach another device: no remote copies, remote signals or barrier semaphores. Data moves between devices by JAX's collectives and lax.ppermute only.
A program may use at most 128 MiB of HBM per device.

```python
import jax
import jax.numpy as jnp
from jax import lax

F_IN = 128
HIDDEN_SIZE = 1024
BLOCK = 128
NODES = 32768
MAXT = 128
N_ROW = 8
N_COL = 32


def slot_layout(key):
    devices = N_ROW * N_COL
    half_cols = N_ROW // 2
    order_key, flip_key = jax.random.split(key)
    device_keys = jax.random.split(order_key, devices)
    order = jax.vmap(lambda k: jax.random.permutation(k, MAXT))(device_keys).astype(jnp.int32)
    flips = jax.random.randint(flip_key, (devices, half_cols), 0, 2).astype(jnp.int32)
    block_row = order // half_cols
    pair_col = order % half_cols
    parity = (block_row % 2 + jnp.take_along_axis(flips, pair_col, axis=1)) % 2
    block_col = 2 * pair_col + parity
    return (block_row.reshape(-1).astype(jnp.int32), block_col.reshape(-1).astype(jnp.int32))


def draw_tile_rows(key, part):
    block_row, block_col = slot_layout(key)
    return block_row


def draw_tile_cols(key, part):
    block_row, block_col = slot_layout(key)
    return block_col


def draw_tile_count(key, part):
    key = jax.random.fold_in(key, 7)
    devices = N_ROW * N_COL
    base_key, high_key, low_key = jax.random.split(key, 3)
    draws = jax.random.randint(base_key, (devices,), 0, MAXT).astype(jnp.int32)
    counts = jnp.minimum(draws * draws // MAXT + MAXT // 8, MAXT)
    high_dev = jax.random.randint(high_key, (), 0, devices).astype(jnp.int32)
    low_dev = (high_dev + 1 + jax.random.randint(low_key, (), 0, devices - 1).astype(jnp.int32)) % devices
    counts = counts.at[high_dev].set(MAXT)
    counts = counts.at[low_dev].set(MAXT // 8)
    return counts.astype(jnp.int32)


def block_scale(rng, extent, cuts, least, high):
    loudness = 1.0
    for position, shards_of in cuts:
        steps = jax.random.uniform(jax.random.fold_in(jax.random.fold_in(rng, 6), position), (shards_of,), jnp.float32, least / len(cuts), high / len(cuts))
        loudness = loudness * jnp.repeat(jnp.exp(steps), extent[position] // shards_of).reshape((-1,) + (1,) * (len(extent) - 1 - position))
    return loudness


def centred(own_key, dims, spread, reach, cuts=(), dtype=jnp.bfloat16):
    factor_of = block_scale(own_key, dims, cuts, -0.22, 0.18) if cuts else 1.0
    result = jax.random.normal(own_key, dims, jnp.float32) * spread * factor_of
    return jnp.minimum(jnp.maximum(result, -reach), reach).astype(dtype)


def setup_inputs(seed: int = 0) -> dict:
    key_list = jax.random.split(jax.random.key(seed), 8)
    features = centred(key_list[0], (NODES, F_IN), 1.0, 6.0, ((0, 256),))
    tile_values = centred(key_list[1], (N_ROW * N_COL * MAXT, BLOCK, BLOCK), (BLOCK * MAXT // 2) ** -0.5, 0.0625, ((0, 256),))
    tile_rows = draw_tile_rows(jax.random.fold_in(key_list[7], 71), 0)
    tile_cols = draw_tile_cols(jax.random.fold_in(key_list[7], 71), 0)
    tile_count = draw_tile_count(jax.random.fold_in(key_list[7], 71), 0)
    weight_in = centred(key_list[5], (F_IN, HIDDEN_SIZE), F_IN ** -0.5, 0.5)
    weight_hidden = centred(key_list[6], (HIDDEN_SIZE, HIDDEN_SIZE), HIDDEN_SIZE ** -0.5, 0.1875)
    return {"features": features, "tile_values": tile_values, "tile_rows": tile_rows, "tile_cols": tile_cols, "tile_count": tile_count, "weight_in": weight_in, "weight_hidden": weight_hidden}


def over_devices(step_fn, total, tile_count):
    blocks = N_ROW * N_COL

    def device_step(dev, acc):
        return lax.fori_loop(0, tile_count[dev], lambda slot, inner: step_fn(dev, slot, inner), acc)

    return lax.fori_loop(0, blocks, device_step, total)


def reference(features, tile_values, tile_rows, tile_cols, tile_count, weight_in, weight_hidden):
    blocks = N_ROW * N_COL
    feature_blocks = features.reshape(blocks, BLOCK, F_IN)

    def place(dev, slot):
        index = (dev * MAXT + slot).astype(jnp.int32)
        row_block = (dev // N_COL) * N_COL + tile_rows[index]
        col_block = (dev % N_COL) * N_ROW + tile_cols[index]
        return index, row_block.astype(jnp.int32), col_block.astype(jnp.int32)

    def first_step(dev, slot, acc):
        index, row_block, col_block = place(dev, slot)
        term = jnp.dot(tile_values[index], feature_blocks[col_block], preferred_element_type=jnp.float32)
        return acc.at[row_block].add(term)

    first_sum = over_devices(first_step, jnp.zeros((blocks, BLOCK, F_IN), jnp.float32), tile_count)
    first_round = first_sum.reshape(NODES, F_IN).astype(jnp.bfloat16)
    hidden_first = jax.nn.relu(jnp.dot(first_round, weight_in, preferred_element_type=jnp.float32)).astype(jnp.bfloat16)
    hidden_blocks = hidden_first.reshape(blocks, BLOCK, HIDDEN_SIZE)

    def second_step(dev, slot, acc):
        index, row_block, col_block = place(dev, slot)
        term = jnp.dot(tile_values[index].T, hidden_blocks[row_block], preferred_element_type=jnp.float32)
        return acc.at[col_block].add(term)

    second_sum = over_devices(second_step, jnp.zeros((blocks, BLOCK, HIDDEN_SIZE), jnp.float32), tile_count)
    second_round = second_sum.reshape(NODES, HIDDEN_SIZE).astype(jnp.bfloat16)
    return jax.nn.relu(jnp.dot(second_round, weight_hidden, preferred_element_type=jnp.float32)).astype(jnp.bfloat16)
```

```python
import functools

import jax
import jax.numpy as jnp
from jax import lax
from jax.experimental import pallas as pl
from jax.experimental.pallas import tpu as pltpu
from jax.sharding import Mesh
from jax.sharding import PartitionSpec as P

NY, NC, NX, NH, NL = 4, 2, 4, 4, 2
NZ = NH * NL
BLOCK = 128
COLS = NY * NC
SIDE = NZ * BLOCK
GROUP = 16
BF = jnp.bfloat16
F32 = jnp.float32


def shift(value, axis, size, step):
    return lax.ppermute(value, axis, [(i, (i + step) % size) for i in range(size)])


def place_kernel(transposed, code, tiles, dense, held, sems):
    groups = held.shape[0] // GROUP

    def load(g):
        part = pl.ds(g * GROUP, GROUP)
        return pltpu.make_async_copy(tiles.at[part], held.at[part], sems.at[g])

    for g in range(groups):
        load(g).start()
    dense[...] = jnp.zeros_like(dense)
    for g in range(groups):
        load(g).wait()
        for slot in range(g * GROUP, (g + 1) * GROUP):
            word = code[slot]
            row_at = lax.shift_right_logical(word, 4) & (NX * NZ - 1)
            col_at = lax.shift_right_logical(word, 1) & (COLS - 1)
            tile = jnp.where((word & 1) == 1, held[slot], jnp.zeros((BLOCK, BLOCK), BF))
            rows = pl.ds(pl.multiple_of(row_at * BLOCK, BLOCK), BLOCK)
            cols = pl.ds(pl.multiple_of(col_at * BLOCK, BLOCK), BLOCK)
            if transposed:
                dense[cols, rows] = tile.T
            else:
                dense[rows, cols] = tile


def place(transposed, code, tiles):
    shape = (NX * SIDE, COLS * BLOCK)
    shape = shape[::-1] if transposed else shape
    return pl.pallas_call(
        functools.partial(place_kernel, transposed),
        in_specs=[
            pl.BlockSpec(memory_space=pltpu.SMEM),
            pl.BlockSpec(memory_space=pltpu.HBM),
        ],
        out_specs=pl.BlockSpec(memory_space=pltpu.VMEM),
        out_shape=jax.ShapeDtypeStruct(shape, BF),
        scratch_shapes=[
            pltpu.VMEM(tiles.shape, BF),
            pltpu.SemaphoreType.DMA((tiles.shape[0] // GROUP,)),
        ],
        compiler_params=pltpu.CompilerParams(vmem_limit_bytes=16 * 2**20),
        cost_estimate=pl.CostEstimate(flops=10**10, bytes_accessed=2**24, transcendentals=0),
        name="place_t" if transposed else "place",
    )(code, pltpu.with_memory_space_constraint(tiles, pltpu.HBM))


def slot_codes(rows, cols, count):
    y, core = lax.axis_index("y"), lax.axis_index("core")
    col_at = ((cols + core) % NC) * NY + (cols // NC - y + NY) % NY
    live = lax.iota(jnp.int32, rows.shape[0]) < count[0]
    low = col_at * 2 + live
    x, z = rows // NZ, rows % NZ
    high, deep = z // NL, z % NL
    sent_at = (x * NL + deep) * NH + (high - lax.axis_index("zh") + NH) % NH
    far = (x - lax.axis_index("x") + NX) % NX
    held_at = jnp.where(far < 2, far, 5 - far) * NZ + z
    return (sent_at * 16 + low).astype(jnp.int32), (held_at * 16 + low).astype(jnp.int32)


def body(features, tile_values, tile_rows, tile_cols, tile_count, weight_in, weight_hidden):
    code, code_t = slot_codes(tile_rows, tile_cols, tile_count)

    pair = jnp.concatenate([features, shift(features, "core", NC, 1)], 0)
    after = {i: shift(pair, "y", NY, (NY - i) % NY) for i in (2, 1, 3)}
    code, after[2] = lax.optimization_barrier((code, after[2]))
    dense = place(False, code, tile_values)
    dense, after[1], after[3] = lax.optimization_barrier((dense, after[1], after[3]))
    near = [pair, after[1], after[2], after[3]]
    column = jnp.concatenate([p[:BLOCK] for p in near] + [p[BLOCK:] for p in near], 0)

    terms = jnp.dot(dense, column, preferred_element_type=F32).astype(BF)
    swapped = lax.all_to_all(terms, ("x", "zl"), 0, 0, tiled=True)
    total = swapped.reshape(NX * NL, NH * BLOCK, -1).astype(F32).sum(0)
    sent = total.astype(BF)
    got = [shift(sent[i * BLOCK : (i + 1) * BLOCK], "zh", NH, i) for i in (2, 1, 3)]
    own = total[:BLOCK] + got[0].astype(F32) + got[1].astype(F32) + got[2].astype(F32)
    own = own.astype(BF)

    own_all = jnp.broadcast_to(own[None], (NZ,) + own.shape).reshape(SIDE, -1)
    near = lax.all_to_all(own_all, ("zh", "zl"), 0, 0, tiled=True)
    code_t, near = lax.optimization_barrier((code_t, near))
    dense_t = place(True, code_t, tile_values)

    def fetch(panel, i):
        return shift(panel, "x", NX, (NX - i) % NX)

    def hidden(panel):
        states = jax.nn.relu(jnp.dot(panel, weight_in, preferred_element_type=F32))
        return lax.optimization_barrier(states.astype(BF))

    def second(rows, cols, states):
        return jnp.dot(dense_t[rows, cols], states, preferred_element_type=F32)

    every = slice(None)
    middle = [fetch(near, 1), fetch(near, 3)]
    states, near = lax.optimization_barrier((hidden(near), near))
    last = fetch(near, 2)
    term = second(every, slice(0, SIDE), states)
    middle = jnp.concatenate(middle, 0)
    term, middle = lax.optimization_barrier((term, middle))
    terms = second(every, slice(SIDE, 3 * SIDE), hidden(middle))
    terms, last = lax.optimization_barrier((terms, last))
    last = hidden(last)
    half = NY * BLOCK
    upper, lower = slice(0, half), slice(half, 2 * half)
    tail = slice(3 * SIDE, 4 * SIDE)
    given = (term[lower] + terms[lower] + second(lower, tail, last)).astype(BF)
    kept = term[upper] + terms[upper] + second(upper, tail, last)
    sums = {}
    for i in (2, 1, 3, 0):
        rows = slice(i * BLOCK, (i + 1) * BLOCK)
        mine = kept[rows] + shift(given[rows], "core", NC, 1).astype(F32)
        sums[i] = shift(mine.astype(BF), "y", NY, i).astype(F32) if i else mine
    own = (sums[0] + sums[2] + sums[1] + sums[3]).astype(BF)
    out = jnp.dot(own, weight_hidden, preferred_element_type=F32)
    return jax.nn.relu(out).astype(BF)


def solution(mesh):
    grid = Mesh(mesh.devices.reshape(NY, NC, NX, NH, NL), ("y", "core", "x", "zh", "zl"))
    nodes, slots = ("x", "zh", "zl", "y", "core"), ("y", "core", "x", "zh", "zl")
    return jax.shard_map(
        body,
        mesh=grid,
        in_specs=(
            P(nodes, None),
            P(slots, None, None),
            P(slots),
            P(slots),
            P(slots),
            P(),
            P(),
        ),
        out_specs=P(nodes, None),
        check_vma=False,
    )
```

```python
import functools

import jax
import jax.numpy as jnp
from jax import lax
from jax.experimental import pallas as pl
from jax.experimental.pallas import tpu as pltpu
from jax.sharding import Mesh
from jax.sharding import PartitionSpec as P

NY, NC, NX, NH, NL = 4, 2, 4, 4, 2
NZ = NH * NL
BLOCK = 128
COLS = NY * NC
SIDE = NZ * BLOCK
GROUP = 16
BF = jnp.bfloat16
F32 = jnp.float32


def shift(value, axis, size, step):
    return lax.ppermute(value, axis, [(i, (i + step) % size) for i in range(size)])


def place_kernel(transposed, code, tiles, dense, held, sems):
    groups = held.shape[0] // GROUP

    def load(g):
        part = pl.ds(g * GROUP, GROUP)
        return pltpu.make_async_copy(tiles.at[part], held.at[part], sems.at[g])

    for g in range(groups):
        load(g).start()
    dense[...] = jnp.zeros_like(dense)
    for g in range(groups):
        load(g).wait()
        for slot in range(g * GROUP, (g + 1) * GROUP):
            word = code[slot]
            row_at = lax.shift_right_logical(word, 12 if transposed else 7) & (NX * NZ - 1)
            col_at = lax.shift_right_logical(word, 4 if transposed else 1) & (COLS - 1)
            tile = jnp.where((word & 1) == 1, held[slot], jnp.zeros((BLOCK, BLOCK), BF))
            rows = pl.ds(pl.multiple_of(row_at * BLOCK, BLOCK), BLOCK)
            cols = pl.ds(pl.multiple_of(col_at * BLOCK, BLOCK), BLOCK)
            if transposed:
                dense[cols, rows] = tile.T
            else:
                dense[rows, cols] = tile


def place(transposed, code, tiles):
    shape = (NX * SIDE, COLS * BLOCK)
    shape = shape[::-1] if transposed else shape
    return pl.pallas_call(
        functools.partial(place_kernel, transposed),
        in_specs=[
            pl.BlockSpec(memory_space=pltpu.SMEM),
            pl.BlockSpec(memory_space=pltpu.HBM),
        ],
        out_specs=pl.BlockSpec(memory_space=pltpu.VMEM),
        out_shape=jax.ShapeDtypeStruct(shape, BF),
        scratch_shapes=[
            pltpu.VMEM(tiles.shape, BF),
            pltpu.SemaphoreType.DMA((tiles.shape[0] // GROUP,)),
        ],
        compiler_params=pltpu.CompilerParams(vmem_limit_bytes=16 * 2**20),
        cost_estimate=pl.CostEstimate(flops=10**10, bytes_accessed=2**24, transcendentals=0),
        name="place_t" if transposed else "place",
    )(code, pltpu.with_memory_space_constraint(tiles, pltpu.HBM))


def slot_codes(rows, cols, count):
    other = (cols + lax.axis_index("core")) % NC
    off = (cols // NC - lax.axis_index("y") + NY) % NY
    live = lax.iota(jnp.int32, rows.shape[0]) < count[0]
    x, z = rows // NZ, rows % NZ
    high, deep = z // NL, z % NL
    sent_at = (x * NL + deep) * NH + high
    far = (x - lax.axis_index("x") + NX) % NX
    z_at = (deep + lax.axis_index("zl")) % NL * NH + high
    held_at = jnp.where(far < 2, far, 5 - far) * NZ + z_at
    late = NC + (1 - other) * (NY - 1) + jnp.where(off == 0, 2, off // 2)
    order = jnp.where(off == 2, 1 - other, late)
    word = (held_at * (NX * NZ) + sent_at) * COLS + order
    return ((word * COLS + other * NY + off) * 2 + live).astype(jnp.int32)


def body(features, tile_values, tile_rows, tile_cols, tile_count, weight_in, weight_hidden):
    code = slot_codes(tile_rows, tile_cols, tile_count)

    pair = jnp.concatenate([features, shift(features, "core", NC, 1)], 0)
    after = {i: shift(pair, "y", NY, (NY - i) % NY) for i in (2, 1, 3)}
    code, after[2] = lax.optimization_barrier((code, after[2]))
    dense = place(False, code, tile_values)
    dense, after[1], after[3] = lax.optimization_barrier((dense, after[1], after[3]))
    near = [pair, after[1], after[2], after[3]]
    column = jnp.concatenate([p[:BLOCK] for p in near] + [p[BLOCK:] for p in near], 0)

    terms = jnp.dot(dense, column, preferred_element_type=F32).astype(BF)
    swapped = lax.all_to_all(terms, ("x", "zl"), 0, 0, tiled=True)
    sent = swapped.reshape(NX * NL, NH * BLOCK, -1).astype(F32).sum(0).astype(BF)
    got = {i: shift(sent, "zh", NH, i) for i in (1, 3, 2)}
    code, got[2] = lax.optimization_barrier((code, got[2]))
    dense_t = place(True, code, tile_values)
    dense_t, got[1], got[3] = lax.optimization_barrier((dense_t, got[1], got[3]))
    own = sent.astype(F32) + got[1].astype(F32) + got[3].astype(F32) + got[2].astype(F32)
    own = own.astype(BF)
    near = jnp.concatenate([own, shift(own, "zl", NL, 1)], 0)

    def fetch(panel, i):
        return shift(panel, "x", NX, (NX - i) % NX)

    def hidden(panel):
        states = jax.nn.relu(jnp.dot(panel, weight_in, preferred_element_type=F32))
        return lax.optimization_barrier(states.astype(BF))

    def second(i, rows, states):
        cols = slice(i * SIDE, (i + 1) * SIDE)
        return jnp.dot(dense_t[rows, cols], states, preferred_element_type=F32)

    every = slice(None)
    one, three = fetch(near, 1), fetch(near, 3)
    states, near = lax.optimization_barrier((hidden(near), near))
    term = second(0, every, states)
    term, one = lax.optimization_barrier((term, one))
    term, three = lax.optimization_barrier((term, three))
    term1 = second(1, every, hidden(one))
    halves = [fetch(one[: SIDE // 2], 1), fetch(three[SIDE // 2 :], 3)]
    two = jnp.concatenate(halves, 0)
    term3 = second(2, every, hidden(three))
    term3, two = lax.optimization_barrier((term3, two))
    two = hidden(two)

    def final(start, count, states):
        rows = slice(start * BLOCK, (start + count) * BLOCK)
        return term[rows] + term1[rows] + term3[rows] + second(3, rows, states)

    def swap(given):
        return shift(given, "core", NC, 1).astype(F32)

    opposite = final(0, NC, two)
    sums = {2: (opposite[BLOCK:] + swap(opposite[:BLOCK].astype(BF))).astype(BF)}
    given = final(NC, NY - 1, two).astype(BF)
    two, given, sums[2] = lax.optimization_barrier((two, given, sums[2]))
    kept = final(NC + NY - 1, NY - 1, two)
    for place_at, i in enumerate((1, 3, 0)):
        rows = slice(place_at * BLOCK, (place_at + 1) * BLOCK)
        sums[i] = kept[rows] + swap(given[rows])
    own = sums[0]
    for i in (2, 1, 3):
        own = own + shift(sums[i].astype(BF), "y", NY, i).astype(F32)
    out = jnp.dot(own.astype(BF), weight_hidden, preferred_element_type=F32)
    return jax.nn.relu(out).astype(BF)


def solution(mesh):
    grid = Mesh(mesh.devices.reshape(NY, NC, NX, NH, NL), ("y", "core", "x", "zh", "zl"))
    nodes, slots = ("x", "zh", "zl", "y", "core"), ("y", "core", "x", "zh", "zl")
    return jax.shard_map(
        body,
        mesh=grid,
        in_specs=(
            P(nodes, None),
            P(slots, None, None),
            P(slots),
            P(slots),
            P(slots),
            P(),
            P(),
        ),
        out_specs=P(nodes, None),
        check_vma=False,
    )
```

```python
import functools

import jax
import jax.numpy as jnp
from jax import lax
from jax.experimental import pallas as pl
from jax.experimental.pallas import tpu as pltpu
from jax.sharding import Mesh
from jax.sharding import PartitionSpec as P

NY, NC, NX, NH, NL = 4, 2, 4, 4, 2
NZ = NH * NL
BLOCK = 128
COLS = NY * NC
SIDE = NZ * BLOCK
GROUP = 16
BF = jnp.bfloat16
F32 = jnp.float32


def shift(value, axis, size, step):
    return lax.ppermute(value, axis, [(i, (i + step) % size) for i in range(size)])


def place_kernel(transposed, code, tiles, dense, held, sems):
    groups = held.shape[0] // GROUP

    def load(g):
        part = pl.ds(g * GROUP, GROUP)
        return pltpu.make_async_copy(tiles.at[part], held.at[part], sems.at[g])

    for g in range(groups):
        load(g).start()
    dense[...] = jnp.zeros_like(dense)
    for g in range(groups):
        load(g).wait()
        for slot in range(g * GROUP, (g + 1) * GROUP):
            word = code[slot]
            row_at = lax.shift_right_logical(word, 12 if transposed else 7) & (NX * NZ - 1)
            col_at = lax.shift_right_logical(word, 4 if transposed else 1) & (COLS - 1)
            tile = jnp.where((word & 1) == 1, held[slot], jnp.zeros((BLOCK, BLOCK), BF))
            rows = pl.ds(pl.multiple_of(row_at * BLOCK, BLOCK), BLOCK)
            cols = pl.ds(pl.multiple_of(col_at * BLOCK, BLOCK), BLOCK)
            if transposed:
                dense[cols, rows] = tile.T
            else:
                dense[rows, cols] = tile


def place(transposed, code, tiles):
    shape = (NX * SIDE, COLS * BLOCK)
    shape = shape[::-1] if transposed else shape
    return pl.pallas_call(
        functools.partial(place_kernel, transposed),
        in_specs=[
            pl.BlockSpec(memory_space=pltpu.SMEM),
            pl.BlockSpec(memory_space=pltpu.HBM),
        ],
        out_specs=pl.BlockSpec(memory_space=pltpu.VMEM),
        out_shape=jax.ShapeDtypeStruct(shape, BF),
        scratch_shapes=[
            pltpu.VMEM(tiles.shape, BF),
            pltpu.SemaphoreType.DMA((tiles.shape[0] // GROUP,)),
        ],
        compiler_params=pltpu.CompilerParams(vmem_limit_bytes=16 * 2**20),
        cost_estimate=pl.CostEstimate(flops=10**10, bytes_accessed=2**24, transcendentals=0),
        name="place_t" if transposed else "place",
    )(code, pltpu.with_memory_space_constraint(tiles, pltpu.HBM))


def slot_codes(rows, cols, count):
    other = (cols + lax.axis_index("core")) % NC
    off = (cols // NC - lax.axis_index("y") + NY) % NY
    live = lax.iota(jnp.int32, rows.shape[0]) < count[0]
    x, z = rows // NZ, rows % NZ
    high, deep = z // NL, z % NL
    far = (x - lax.axis_index("x") + NX) % NX
    beside = (deep + lax.axis_index("zl")) % NL
    sent_at = (far * NL + beside) * NH + high
    z_at = beside * NH + high
    held_at = jnp.where(far < 2, far, 5 - far) * NZ + z_at
    late = NC + (1 - other) * (NY - 1) + jnp.where(off == 0, 2, off // 2)
    order = jnp.where(off == 2, 1 - other, late)
    word = (held_at * (NX * NZ) + sent_at) * COLS + order
    return ((word * COLS + other * NY + off) * 2 + live).astype(jnp.int32)


def body(features, tile_values, tile_rows, tile_cols, tile_count, weight_in, weight_hidden):
    code = slot_codes(tile_rows, tile_cols, tile_count)

    pair = jnp.concatenate([features, shift(features, "core", NC, 1)], 0)
    after = {i: shift(pair, "y", NY, (NY - i) % NY) for i in (2, 1, 3)}
    code, after[2] = lax.optimization_barrier((code, after[2]))
    dense = place(False, code, tile_values)
    dense, after[1], after[3] = lax.optimization_barrier((dense, after[1], after[3]))
    near = [pair, after[1], after[2], after[3]]
    column = jnp.concatenate([p[:BLOCK] for p in near] + [p[BLOCK:] for p in near], 0)

    terms = jnp.dot(dense, column, preferred_element_type=F32).astype(BF)
    part = NH * BLOCK
    total = terms[:part].astype(F32)
    for a, b in ((2, 1), (2, 0), (1, 1), (3, 1), (1, 0), (3, 0), (0, 1)):
        start = (a * NL + b) * part
        ring = [((i + a) % NX) * NL + (j + b) % NL for i in range(NX) for j in range(NL)]
        total += lax.ppermute(terms[start : start + part], ("x", "zl"), list(enumerate(ring))).astype(F32)
    sent = total.astype(BF)
    got = {i: shift(sent, "zh", NH, i) for i in (1, 3, 2)}
    code, got[2] = lax.optimization_barrier((code, got[2]))
    dense_t = place(True, code, tile_values)
    dense_t, got[1], got[3] = lax.optimization_barrier((dense_t, got[1], got[3]))
    own = sent.astype(F32) + got[1].astype(F32) + got[3].astype(F32) + got[2].astype(F32)
    own = own.astype(BF)
    near = jnp.concatenate([own, shift(own, "zl", NL, 1)], 0)

    def fetch(panel, i):
        return shift(panel, "x", NX, (NX - i) % NX)

    def hidden(panel):
        states = jax.nn.relu(jnp.dot(panel, weight_in, preferred_element_type=F32))
        return lax.optimization_barrier(states.astype(BF))

    def second(i, rows, states):
        cols = slice(i * SIDE, (i + 1) * SIDE)
        return jnp.dot(dense_t[rows, cols], states, preferred_element_type=F32)

    every = slice(None)
    one, three = fetch(near, 1), fetch(near, 3)
    states, near = lax.optimization_barrier((hidden(near), near))
    term = second(0, every, states)
    term, one = lax.optimization_barrier((term, one))
    term, three = lax.optimization_barrier((term, three))
    term1 = second(1, every, hidden(one))
    halves = [fetch(one[: SIDE // 2], 1), fetch(three[SIDE // 2 :], 3)]
    two = jnp.concatenate(halves, 0)
    term3 = second(2, every, hidden(three))
    term3, two = lax.optimization_barrier((term3, two))
    two = hidden(two)

    def final(start, count, states):
        rows = slice(start * BLOCK, (start + count) * BLOCK)
        return term[rows] + term1[rows] + term3[rows] + second(3, rows, states)

    def swap(given):
        return shift(given, "core", NC, 1).astype(F32)

    opposite = final(0, NC, two)
    sums = {2: (opposite[BLOCK:] + swap(opposite[:BLOCK].astype(BF))).astype(BF)}
    given = final(NC, NY - 1, two).astype(BF)
    two, given, sums[2] = lax.optimization_barrier((two, given, sums[2]))
    kept = final(NC + NY - 1, NY - 1, two)
    for place_at, i in enumerate((1, 3, 0)):
        rows = slice(place_at * BLOCK, (place_at + 1) * BLOCK)
        sums[i] = kept[rows] + swap(given[rows])
    own = sums[0]
    for i in (2, 1, 3):
        own = own + shift(sums[i].astype(BF), "y", NY, i).astype(F32)
    out = jnp.dot(own.astype(BF), weight_hidden, preferred_element_type=F32)
    return jax.nn.relu(out).astype(BF)


def solution(mesh):
    grid = Mesh(mesh.devices.reshape(NY, NC, NX, NH, NL), ("y", "core", "x", "zh", "zl"))
    nodes, slots = ("x", "zh", "zl", "y", "core"), ("y", "core", "x", "zh", "zl")
    return jax.shard_map(
        body,
        mesh=grid,
        in_specs=(
            P(nodes, None),
            P(slots, None, None),
            P(slots),
            P(slots),
            P(slots),
            P(),
            P(),
        ),
        out_specs=P(nodes, None),
        check_vma=False,
    )
```

```python
import functools

import jax
import jax.numpy as jnp
from jax import lax
from jax.experimental import pallas as pl
from jax.experimental.pallas import tpu as pltpu
from jax.sharding import Mesh
from jax.sharding import PartitionSpec as P

NY, NC, NX, NH, NL = 4, 2, 4, 4, 2
NZ = NH * NL
BLOCK = 128
COLS = NY * NC
SIDE = NZ * BLOCK
GROUP = 16
BF = jnp.bfloat16
F32 = jnp.float32


def shift(value, axis, size, step):
    return lax.ppermute(value, axis, [(i, (i + step) % size) for i in range(size)])


def place_kernel(transposed, code, tiles, dense, held, sems):
    groups = held.shape[0] // GROUP

    def load(g):
        part = pl.ds(g * GROUP, GROUP)
        return pltpu.make_async_copy(tiles.at[part], held.at[part], sems.at[g])

    for g in range(groups):
        load(g).start()
    dense[...] = jnp.zeros_like(dense)
    for g in range(groups):
        load(g).wait()
        for slot in range(g * GROUP, (g + 1) * GROUP):
            word = code[slot]
            row_at = lax.shift_right_logical(word, 12 if transposed else 7) & (NX * NZ - 1)
            col_at = lax.shift_right_logical(word, 4 if transposed else 1) & (COLS - 1)
            tile = jnp.where((word & 1) == 1, held[slot], jnp.zeros((BLOCK, BLOCK), BF))
            rows = pl.ds(pl.multiple_of(row_at * BLOCK, BLOCK), BLOCK)
            cols = pl.ds(pl.multiple_of(col_at * BLOCK, BLOCK), BLOCK)
            if transposed:
                dense[cols, rows] = tile.T
            else:
                dense[rows, cols] = tile


def place(transposed, code, tiles):
    shape = (NX * SIDE, COLS * BLOCK)
    shape = shape[::-1] if transposed else shape
    return pl.pallas_call(
        functools.partial(place_kernel, transposed),
        in_specs=[
            pl.BlockSpec(memory_space=pltpu.SMEM),
            pl.BlockSpec(memory_space=pltpu.HBM),
        ],
        out_specs=pl.BlockSpec(memory_space=pltpu.VMEM),
        out_shape=jax.ShapeDtypeStruct(shape, BF),
        scratch_shapes=[
            pltpu.VMEM(tiles.shape, BF),
            pltpu.SemaphoreType.DMA((tiles.shape[0] // GROUP,)),
        ],
        compiler_params=pltpu.CompilerParams(vmem_limit_bytes=16 * 2**20),
        cost_estimate=pl.CostEstimate(flops=10**10, bytes_accessed=2**24, transcendentals=0),
        name="place_t" if transposed else "place",
    )(code, pltpu.with_memory_space_constraint(tiles, pltpu.HBM))


def slot_codes(rows, cols, count):
    other = (cols + lax.axis_index("core")) % NC
    off = (cols // NC - lax.axis_index("y") + NY) % NY
    live = lax.iota(jnp.int32, rows.shape[0]) < count[0]
    x, z = rows // NZ, rows % NZ
    high, deep = z // NL, z % NL
    far = (x - lax.axis_index("x") + NX) % NX
    beside = (deep + lax.axis_index("zl")) % NL
    sent_at = (far * NL + beside) * NH + high
    half = jnp.where(far % 2 == 0, far * 3 + beside, 2 + far // 2 + beside * 2)
    held_at = half * NH + high
    late = NC + (1 - other) * (NY - 1) + jnp.where(off == 0, 2, off // 2)
    order = jnp.where(off == 2, 1 - other, late)
    word = (held_at * (NX * NZ) + sent_at) * COLS + order
    return ((word * COLS + other * NY + off) * 2 + live).astype(jnp.int32)


def body(features, tile_values, tile_rows, tile_cols, tile_count, weight_in, weight_hidden):
    code = slot_codes(tile_rows, tile_cols, tile_count)

    pair = jnp.concatenate([features, shift(features, "core", NC, 1)], 0)
    after = {i: shift(pair, "y", NY, (NY - i) % NY) for i in (2, 1, 3)}
    code, after[2] = lax.optimization_barrier((code, after[2]))
    dense = place(False, code, tile_values)
    dense, after[1], after[3] = lax.optimization_barrier((dense, after[1], after[3]))
    near = [pair, after[1], after[2], after[3]]
    column = jnp.concatenate([p[:BLOCK] for p in near] + [p[BLOCK:] for p in near], 0)

    terms = jnp.dot(dense, column, preferred_element_type=F32).astype(BF)
    part = NH * BLOCK
    total = terms[:part].astype(F32)
    for a, b in ((2, 1), (2, 0), (1, 1), (3, 1), (1, 0), (3, 0), (0, 1)):
        start = (a * NL + b) * part
        ring = [((i + a) % NX) * NL + (j + b) % NL for i in range(NX) for j in range(NL)]
        total += lax.ppermute(terms[start : start + part], ("x", "zl"), list(enumerate(ring))).astype(F32)
    sent = total.astype(BF)
    got = {i: shift(sent, "zh", NH, i) for i in (1, 3, 2)}
    code, got[2] = lax.optimization_barrier((code, got[2]))
    dense_t = place(True, code, tile_values)
    dense_t, got[1], got[3] = lax.optimization_barrier((dense_t, got[1], got[3]))
    own = sent.astype(F32) + got[1].astype(F32) + got[3].astype(F32) + got[2].astype(F32)
    own = own.astype(BF)
    def fetch(own, a, b):
        ring = [((i - a) % NX) * NL + (j - b) % NL for i in range(NX) for j in range(NL)]
        return lax.ppermute(own, ("x", "zl"), list(enumerate(ring)))

    def hidden(panel):
        states = jax.nn.relu(jnp.dot(panel, weight_in, preferred_element_type=F32))
        return lax.optimization_barrier(states.astype(BF))

    def second(i, rows, states):
        cols = slice(i * SIDE, (i + 1) * SIDE)
        return jnp.dot(dense_t[rows, cols], states, preferred_element_type=F32)

    every = slice(None)
    near, pair = [own, fetch(own, 0, 1)], [fetch(own, 1, 0), fetch(own, 3, 0)]
    states, own = lax.optimization_barrier((hidden(jnp.concatenate(near, 0)), own))
    beside = [fetch(own, 1, 1), fetch(own, 3, 1)]
    term = second(0, every, states)
    term, pair, own = lax.optimization_barrier((term, pair, own))
    distant = [fetch(own, 2, 0), fetch(own, 2, 1)]
    term1 = second(1, every, hidden(jnp.concatenate(pair, 0)))
    term1, beside = lax.optimization_barrier((term1, beside))
    term3 = second(2, every, hidden(jnp.concatenate(beside, 0)))
    term3, distant = lax.optimization_barrier((term3, distant))
    two = hidden(jnp.concatenate(distant, 0))

    def final(start, count, states):
        rows = slice(start * BLOCK, (start + count) * BLOCK)
        return term[rows] + term1[rows] + term3[rows] + second(3, rows, states)

    def swap(given):
        return shift(given, "core", NC, 1).astype(F32)

    opposite = final(0, NC, two)
    sums = {2: (opposite[BLOCK:] + swap(opposite[:BLOCK].astype(BF))).astype(BF)}
    given = final(NC, NY - 1, two).astype(BF)
    two, given, sums[2] = lax.optimization_barrier((two, given, sums[2]))
    kept = final(NC + NY - 1, NY - 1, two)
    for place_at, i in enumerate((1, 3, 0)):
        rows = slice(place_at * BLOCK, (place_at + 1) * BLOCK)
        sums[i] = kept[rows] + swap(given[rows])
    own = sums[0]
    for i in (2, 1, 3):
        own = own + shift(sums[i].astype(BF), "y", NY, i).astype(F32)
    out = jnp.dot(own.astype(BF), weight_hidden, preferred_element_type=F32)
    return jax.nn.relu(out).astype(BF)


def solution(mesh):
    grid = Mesh(mesh.devices.reshape(NY, NC, NX, NH, NL), ("y", "core", "x", "zh", "zl"))
    nodes, slots = ("x", "zh", "zl", "y", "core"), ("y", "core", "x", "zh", "zl")
    return jax.shard_map(
        body,
        mesh=grid,
        in_specs=(
            P(nodes, None),
            P(slots, None, None),
            P(slots),
            P(slots),
            P(slots),
            P(),
            P(),
        ),
        out_specs=P(nodes, None),
        check_vma=False,
    )
```
